512 devices in a mesh: dp: 16 (over y, z_hi, core), feat: 32 (over z_lo, x).
Axes of the slice: x: 4, y: 4, z: 16 (z_hi: 2, z_lo: 8; z = z_hi * 8 + z_lo), core: 2. Of those that a mesh axis runs over, the one named last changes fastest.
Arguments:
- inputs: bfloat16 [4096, 16384], P('dp', 'feat'), may hold values from -6 to 6
- cotangent: bfloat16 [4096, 16384], P('dp', 'feat'), may hold values from -6 to 6
- butterfly: bfloat16 [6, 16384, 512], P(None, ('feat', 'dp')), may hold values from -0.109375 to 0.109375
- low_in: bfloat16 [16384, 256], P(('feat', 'dp')), may hold values from -0.046875 to 0.046875
- low_out: bfloat16 [256, 16384], P(None, ('feat', 'dp')), may hold values from -0.375 to 0.375
Outputs:
- output: bfloat16 [4096, 16384], P('dp', 'feat')
- grad_inputs: bfloat16 [4096, 16384], P('dp', 'feat')
- grad_butterfly: float32 [6, 16384, 512], P(None, ('feat', 'dp'))
- grad_low_in: float32 [16384, 256], P(('feat', 'dp'))
- grad_low_out: float32 [256, 16384], P(None, ('feat', 'dp'))
The draws below stay inside these ranges and needn't reach their ends.
All inputs are finite; a program needn't handle non-finite values.
Results may differ from the reference program's by a relative error of at most 0.015.
Values may be sent and summed in bfloat16 or wider, within the bound.
No kernel may reach another device: no remote copies, remote signals or barrier semaphores. Data moves between devices by JAX's collectives and lax.ppermute only.
A program may use at most 64 MiB of HBM per device.

```python
import math
import jax
import jax.numpy as jnp
from jax import lax

D = 16384
BS = 512
R = 256
LEVELS = 5
TOK_DEV = 256
TOKENS = 4096
N_DP = 16


def level_of(key, shape, cuts, smallest, high):
    factor_of = 1.0
    for dim, parts in cuts:
        steps = jax.random.uniform(jax.random.fold_in(jax.random.fold_in(key, 6), dim), (parts,), jnp.float32, smallest / len(cuts), high / len(cuts))
        factor_of = factor_of * jnp.repeat(jnp.exp(steps), shape[dim] // parts).reshape((-1,) + (1,) * (len(shape) - 1 - dim))
    return factor_of


def normal_values(stream_key, shape, scale, most, cuts=(), kind=jnp.bfloat16):
    loudness = level_of(stream_key, shape, cuts, -0.22, 0.18) if cuts else 1.0
    values = jax.random.normal(stream_key, shape, jnp.float32) * scale * loudness
    return jnp.minimum(jnp.maximum(values, -most), most).astype(kind)


def setup_inputs(seed: int = 0) -> dict:
    streams_of = jax.random.split(jax.random.key(seed), 6)
    inputs = normal_values(streams_of[0], (TOKENS, D), 1.0, 6.0, ((0, 16), (1, 32)))
    cotangent = normal_values(streams_of[1], (TOKENS, D), 1.0, 6.0, ((0, 16), (1, 32)))
    butterfly = normal_values(streams_of[2], (LEVELS + 1, D, BS), ((LEVELS + 1) * BS) ** -0.5, 0.109375, ((1, 512),))
    low_in = normal_values(streams_of[3], (D, R), D ** -0.5, 0.046875, ((0, 512),))
    low_out = normal_values(streams_of[4], (R, D), R ** -0.5, 0.375, ((1, 512),))
    return {"inputs": inputs, "cotangent": cotangent, "butterfly": butterfly, "low_in": low_in, "low_out": low_out}


def flip_blocks(values, level, lead):
    shape = values.shape
    count = shape[lead]
    split = shape[:lead] + (count >> level + 1, 2, 1 << level) + shape[lead + 1:]
    return jnp.flip(values.reshape(split), lead + 1).reshape(shape)

def forward_mul(left, weights):
    return jnp.einsum('tnr,nrc->tnc', left.astype(jnp.float32), weights.astype(jnp.float32))

def backward_mul(left, weights):
    return jnp.einsum('tnc,nrc->tnr', left.astype(jnp.float32), weights.astype(jnp.float32))

def group_sum(partial_terms, factor):
    rounded = lax.optimization_barrier((partial_terms * factor).astype(jnp.bfloat16))
    return lax.optimization_barrier(jnp.sum(rounded.astype(jnp.float32), axis=0))

def reference(inputs, cotangent, butterfly, low_in, low_out):
    blocks = D // BS
    factor = 1.0 / math.sqrt(TOKENS)
    in_blocks = inputs.reshape(TOKENS, blocks, BS)
    cot_blocks = cotangent.reshape(TOKENS, blocks, BS)
    weight_blocks = butterfly.reshape(LEVELS + 1, blocks, BS, BS)
    low_s = jnp.dot(inputs, low_in, preferred_element_type=jnp.float32).astype(jnp.bfloat16)
    low_t = lax.dot_general(cotangent, low_out, (((1,), (1,)), ((), ())), preferred_element_type=jnp.float32).astype(jnp.bfloat16)
    result = forward_mul(in_blocks, weight_blocks[0])
    partners = [in_blocks]
    for level in range(LEVELS):
        near = flip_blocks(in_blocks, level, 1)
        partners.append(near)
        result = result + forward_mul(near, weight_blocks[level + 1])
    result = result.reshape(TOKENS, D) + jnp.dot(low_s, low_out, preferred_element_type=jnp.float32)
    output = result.astype(jnp.bfloat16)
    back = backward_mul(cot_blocks, weight_blocks[0])
    for level in range(LEVELS):
        term = backward_mul(cot_blocks, weight_blocks[level + 1]).astype(jnp.bfloat16)
        back = back + flip_blocks(term, level, 1).astype(jnp.float32)
    back = back.reshape(TOKENS, D) + lax.dot_general(low_t, low_in, (((1,), (1,)), ((), ())), preferred_element_type=jnp.float32)
    grad_inputs = back.astype(jnp.bfloat16)
    cot_groups = cot_blocks.reshape(N_DP, TOK_DEV, blocks, BS).astype(jnp.float32)
    grads = []
    for level in range(LEVELS + 1):
        left = partners[level].reshape(N_DP, TOK_DEV, blocks, BS).astype(jnp.float32)
        partial_terms = jnp.einsum('gtnr,gtnc->gnrc', left, cot_groups)
        grads.append(group_sum(partial_terms, factor).reshape(D, BS))
    grad_butterfly = jnp.stack(grads)
    in_groups = inputs.reshape(N_DP, TOK_DEV, D).astype(jnp.float32)
    t_groups = low_t.reshape(N_DP, TOK_DEV, R).astype(jnp.float32)
    s_groups = low_s.reshape(N_DP, TOK_DEV, R).astype(jnp.float32)
    grad_low_in = group_sum(jnp.einsum('gtd,gtr->gdr', in_groups, t_groups), factor)
    grad_low_out = group_sum(jnp.einsum('gtr,gtd->grd', s_groups, cotangent.reshape(N_DP, TOK_DEV, D).astype(jnp.float32)), factor)
    return (output, grad_inputs, grad_butterfly, grad_low_in, grad_low_out)
```

```python
import functools

import jax
import jax.numpy as jnp
from jax import lax
from jax.experimental import pallas as pl
from jax.experimental.pallas import tpu as pltpu
from jax.sharding import PartitionSpec as P

BS = 512
LEVELS = 5
R = 256
SCALE = 1.0 / 64.0
F32 = jnp.float32
BF16 = jnp.bfloat16


def dp_pairs(step):
    pairs = []
    for i in range(16):
        y, h, c = step(i // 4, (i // 2) % 2, i % 2)
        pairs.append((i, (y * 2 + h) * 2 + c))
    return pairs


CORE = dp_pairs(lambda y, h, c: (y, h, 1 - c))
Z_HI = dp_pairs(lambda y, h, c: (y, 1 - h, c))
Y_STEP = [dp_pairs(lambda y, h, c, k=k: ((y + k) % 4, h, c)) for k in range(4)]
X_STEP = [[(i, (i // 4) * 4 + (i % 4 + k) % 4) for i in range(32)] for k in range(4)]
PARTNER = [[(i, i ^ (1 << level)) for i in range(32)] for level in range(LEVELS)]
CORE_GROUPS = [[2 * i, 2 * i + 1] for i in range(8)]


def over_dp(value, pairs):
    return lax.ppermute(value, "dp", pairs)


def over_feat(value, pairs):
    return lax.ppermute(value, "feat", pairs)


def dot_nn(a, b):
    return lax.dot_general(a, b, (((1,), (0,)), ((), ())), preferred_element_type=F32)


def dot_nt(a, b):
    return lax.dot_general(a, b, (((1,), (1,)), ((), ())), preferred_element_type=F32)


def dot_tn(a, b):
    return lax.dot_general(a, b, (((0,), (0,)), ((), ())), preferred_element_type=F32)


def call(kernel, out, place, *args, scratch=(), name, limit=24):
    shapes = [jax.ShapeDtypeStruct(s, d) for s, d in out]
    return pl.pallas_call(
        kernel,
        out_shape=shapes,
        in_specs=[pl.BlockSpec(memory_space=pltpu.SMEM)]
        + [pl.BlockSpec(memory_space=pltpu.VMEM)] * len(args),
        out_specs=[pl.BlockSpec(memory_space=pltpu.VMEM)] * len(out),
        scratch_shapes=list(scratch),
        compiler_params=pltpu.CompilerParams(vmem_limit_bytes=limit << 20),
        name=name,
    )(place, *args)


def chunk_of(place, y, h, c):
    return c * 4 + lax.rem(place[0] - y + 4, 4), lax.rem(place[1] + h, 2)


def rows_of(place, k, g, c):
    y = lax.rem(place[0] + k, 4)
    h = lax.rem(place[1] + g, 2)
    return pl.multiple_of(((y * 2 + h) * 2 + c) * 32, 32)


def project_kernel(place, gathered, inputs, cot, low, p0, p1, p2, p3, part):
    for d in range(16):
        i, j = chunk_of(place, d // 4, (d // 2) % 2, d % 2)
        low[d * 32 : (d + 1) * 32, :] = gathered[i, j]
    part[:, :R] = dot_nn(inputs[...], low[:, :R])
    part[:, R:] = dot_nn(cot[...], low[:, R:])
    for k, out in enumerate((p0, p1, p2, p3)):
        row = pl.multiple_of(lax.rem(place[3] + k, 4) * 64, 64)
        out[...] = part[pl.ds(row, 64), :].astype(out.dtype)


def weights_kernel(place, gathered, inputs, near0, near1, cot, z, back, front, far, w):
    for d in range(16):
        i, j = chunk_of(place, d // 4, (d // 2) % 2, d % 2)
        w[:, d * 32 : (d + 1) * 32, :] = gathered[i, j]
    for level in range(LEVELS):
        z[level] = dot_nt(cot[...], w[level + 1]).astype(BF16)
    back[...] = dot_nt(cot[...], w[0])
    front[...] = dot_nn(inputs[...], w[0]) + dot_nn(near0[...], w[1]) + dot_nn(near1[...], w[2])
    far[...] = w[3:]


def split_rows(place, grad, n, keep, send):
    for k in range(4):
        for g in range(2):
            keep[k, g, n] = grad[pl.ds(rows_of(place, k, g, place[2]), 32), :].astype(BF16)
            send[k, g, n] = grad[pl.ds(rows_of(place, k, g, 1 - place[2]), 32), :].astype(BF16)


def near_grads_kernel(place, inputs, near0, near1, cot, keep, send, grad):
    for n, left in enumerate((inputs, near0, near1)):
        grad[...] = dot_tn(left[...], cot[...])
        split_rows(place, grad, n, keep, send)


def far_grads_kernel(
    place, far0, far1, far2, inputs, cot, st0, st1, st2, st3, keep, send, st, grad
):
    for k, part in enumerate((st0, st1, st2, st3)):
        row = pl.multiple_of(lax.rem(place[3] + 4 - k, 4) * 64, 64)
        st[pl.ds(row, 64), :] = part[...]
    for n, left in enumerate((far0, far1, far2)):
        grad[...] = dot_tn(left[...], cot[...])
        split_rows(place, grad, n, keep, send)
    grad[:, :R] = dot_tn(inputs[...], st[:, R:])
    grad[:, R:] = dot_tn(cot[...], st[:, :R])
    split_rows(place, grad, 3, keep, send)


def core_sum_kernel(place, keep, got, q0, q1, q2, q3):
    for k, out in enumerate((q0, q1, q2, q3)):
        out[...] = (keep[k].astype(F32) + got[k].astype(F32)).astype(out.dtype)


def y_sum_kernel(place, q0, q1, q2, q3, mine, send):
    total = q0[...] + q1[...].astype(F32) + q2[...].astype(F32) + q3[...].astype(F32)
    mine[...] = total[0]
    send[...] = total[1].astype(BF16)


def output_kernel(place, front, far0, far1, far2, w, st, low, out):
    total = front[...] + dot_nt(st[:, :R], low[:, R:])
    for n, left in enumerate((far0, far1, far2)):
        total = total + dot_nn(left[...], w[n])
    out[...] = total.astype(BF16)


def grad_inputs_kernel(place, back, z0, z1, z2, z3, z4, st, low, out):
    total = back[...] + dot_nt(st[:, R:], low[:, :R])
    for z in (z0, z1, z2, z3, z4):
        total = total + z[...].astype(F32)
    out[...] = total.astype(BF16)


def reduce_rows(place, kernel, args, n, scratch, name):
    half = (4, 2, n, 32, BS)
    quarter = (2, n, 32, BS)
    extra = call(
        kernel, [(half, BF16)] * 2 + scratch, place, *args,
        scratch=[pltpu.VMEM((BS, BS), F32)], name=name,
    )
    keep, send = extra[:2]
    got = over_dp(send, CORE)
    q = call(core_sum_kernel, [(quarter, F32)] + [(quarter, BF16)] * 3, place, keep, got,
             name=name + "_core")
    r = [over_dp(q[k], Y_STEP[k]) for k in (1, 2, 3)]
    mine, far = call(y_sum_kernel, [(quarter[1:], F32), (quarter[1:], BF16)], place, q[0], *r,
                     name=name + "_y")
    got = over_dp(far, Z_HI)
    return (mine + got.astype(F32)) * SCALE, extra[2:]


def gather_rows(shard):
    pair = jnp.stack([shard, over_dp(shard, Z_HI)])
    steps = [pair] + [over_dp(pair, Y_STEP[k]) for k in (1, 2, 3)]
    return lax.all_gather(
        jnp.stack(steps), "dp", axis=0, tiled=True, axis_index_groups=CORE_GROUPS
    )


def body(inputs, cotangent, butterfly, low_in, low_out):
    dp = lax.axis_index("dp")
    place = jnp.stack([dp // 4, (dp // 2) % 2, dp % 2, lax.axis_index("feat") % 4]).astype(jnp.int32)
    low_all = gather_rows(jnp.concatenate([low_in, low_out.T], axis=1))
    w_all = gather_rows(butterfly)
    near = [over_feat(inputs, PARTNER[level]) for level in range(LEVELS)]

    piece = (64, 2 * R)
    low, *parts = call(
        project_kernel, [((BS, 2 * R), BF16), (piece, F32)] + [(piece, BF16)] * 3,
        place, low_all, inputs, cotangent,
        scratch=[pltpu.VMEM((256, 2 * R), F32)], name="project",
    )
    total = parts[0]
    for k in (1, 2, 3):
        total = total + over_feat(parts[k], X_STEP[k]).astype(F32)
    total = total.astype(BF16)
    for level in (2, 3, 4):
        total = (total.astype(F32) + over_feat(total, PARTNER[level]).astype(F32)).astype(BF16)
    st_parts = [total] + [over_feat(total, X_STEP[k]) for k in (1, 2, 3)]

    block = (256, BS)
    z, back, front, w_far = call(
        weights_kernel,
        [((LEVELS,) + block, BF16), (block, F32), (block, F32), ((3, BS, BS), BF16)],
        place, w_all, inputs, near[0], near[1], cotangent,
        scratch=[pltpu.VMEM((LEVELS + 1, BS, BS), BF16)], name="weights",
    )
    z_near = [over_feat(z[level], PARTNER[level]) for level in range(LEVELS)]

    grads_a, _ = reduce_rows(
        place, near_grads_kernel, (inputs, near[0], near[1], cotangent), 3, [], "near_grads"
    )
    grads_b, (st,) = reduce_rows(
        place, far_grads_kernel, (near[2], near[3], near[4], inputs, cotangent, *st_parts), 4,
        [((256, 2 * R), BF16)], "far_grads",
    )
    (output,) = call(
        output_kernel, [(block, BF16)], place, front, near[2], near[3], near[4], w_far, st, low,
        name="output",
    )
    (grad_inputs,) = call(
        grad_inputs_kernel, [(block, BF16)], place, back, *z_near, st, low, name="grad_inputs"
    )
    grad_butterfly = jnp.concatenate([grads_a, grads_b[:3]], axis=0)
    return output, grad_inputs, grad_butterfly, grads_b[3, :, :R], grads_b[3, :, R:].T


def solution(mesh):
    specs = (
        P("dp", "feat"),
        P("dp", "feat"),
        P(None, ("feat", "dp"), None),
        P(("feat", "dp"), None),
        P(None, ("feat", "dp")),
    )
    return jax.shard_map(body, mesh=mesh, in_specs=specs, out_specs=specs, check_vma=False)
```

```python
import functools

import jax
import jax.numpy as jnp
from jax import lax
from jax.experimental import pallas as pl
from jax.experimental.pallas import tpu as pltpu
from jax.sharding import PartitionSpec as P

BS = 512
LEVELS = 5
R = 256
SCALE = 1.0 / 64.0
F32 = jnp.float32
BF16 = jnp.bfloat16


def dp_pairs(step):
    pairs = []
    for i in range(16):
        y, h, c = step(i // 4, (i // 2) % 2, i % 2)
        pairs.append((i, (y * 2 + h) * 2 + c))
    return pairs


CORE = dp_pairs(lambda y, h, c: (y, h, 1 - c))
Z_HI = dp_pairs(lambda y, h, c: (y, 1 - h, c))
Y_GROUPS = [[(y * 2 + h) * 2 + c for y in range(4)] for h in range(2) for c in range(2)]
YC_GROUPS = [[(y * 2 + h) * 2 + c for y in range(4) for c in range(2)] for h in range(2)]
X_GROUPS = [[z * 4 + x for x in range(4)] for z in range(8)]
PARTNER = [[(i, i ^ (1 << level)) for i in range(32)] for level in range(LEVELS)]


def tie(value, *earlier):
    return lax.optimization_barrier((value, *earlier))[0]


def over_dp(value, pairs):
    return lax.ppermute(value, "dp", pairs)


def over_feat(value, pairs):
    return lax.ppermute(value, "feat", pairs)


def exchange(value, axis, groups):
    return lax.all_to_all(value, axis, 0, 0, tiled=True, axis_index_groups=groups)


def dot_nn(a, b):
    return lax.dot_general(a, b, (((1,), (0,)), ((), ())), preferred_element_type=F32)


def dot_nt(a, b):
    return lax.dot_general(a, b, (((1,), (1,)), ((), ())), preferred_element_type=F32)


def dot_tn(a, b):
    return lax.dot_general(a, b, (((0,), (0,)), ((), ())), preferred_element_type=F32)


def call(kernel, out, place, *args, scratch=(), name, limit=24):
    shapes = [jax.ShapeDtypeStruct(s, d) for s, d in out]
    return pl.pallas_call(
        kernel,
        out_shape=shapes,
        in_specs=[pl.BlockSpec(memory_space=pltpu.SMEM)]
        + [pl.BlockSpec(memory_space=pltpu.VMEM)] * len(args),
        out_specs=[pl.BlockSpec(memory_space=pltpu.VMEM)] * len(out),
        scratch_shapes=list(scratch),
        compiler_params=pltpu.CompilerParams(vmem_limit_bytes=limit << 20),
        name=name,
    )(place, *args)


def rows_of(place, y, g, c):
    h = lax.rem(place[1] + g, 2)
    return pl.multiple_of(((y * 2 + h) * 2 + c) * 32, 32)


def pair_kernel(place, mine, got, weights, low):
    weights[0] = mine[: LEVELS + 1]
    weights[1] = got[: LEVELS + 1]
    for k in range(8):
        low[k, 0] = mine[LEVELS + 1]
        low[k, 1] = got[LEVELS + 1]


def project_kernel(place, gathered, inputs, cot, low, out, part):
    for k in range(8):
        for g in range(2):
            low[pl.ds(rows_of(place, k // 2, g, k % 2), 32), :] = gathered[k, g]
    part[:, :R] = dot_nn(inputs[...], low[:, :R])
    part[:, R:] = dot_nn(cot[...], low[:, R:])
    for x in range(4):
        out[x] = part[x * 64 : (x + 1) * 64, :].astype(BF16)


def weights_kernel(place, gathered, cot, z0, z1, z2, z3, z4, w):
    for k in range(8):
        for g in range(2):
            w[:, pl.ds(rows_of(place, k // 2, g, k % 2), 32), :] = gathered[k, g]
    for level, z in enumerate((z0, z1, z2, z3, z4)):
        z[...] = dot_nt(cot[...], w[level + 1]).astype(BF16)


def x_sum_kernel(place, parts, out):
    total = parts[0].astype(F32)
    for x in range(1, 4):
        total = total + parts[x].astype(F32)
    out[...] = total.astype(BF16)


def near_grads_kernel(place, inputs, n0, n1, cot, out, grad):
    for n, left in enumerate((inputs, n0, n1)):
        grad[...] = dot_tn(left[...], cot[...])
        for k in range(8):
            for g in range(2):
                row = rows_of(place, k // 2, g, k % 2)
                out[k, g, n] = grad[pl.ds(row, 32), :].astype(BF16)


def far_grads_kernel(place, n2, n3, n4, st, inputs, cot, keep, send, grad):
    for n, left in enumerate((n2, n3, n4, None)):
        if left is None:
            grad[:, :R] = dot_tn(inputs[...], st[:, R:])
            grad[:, R:] = dot_tn(cot[...], st[:, :R])
        else:
            grad[...] = dot_tn(left[...], cot[...])
        for y in range(4):
            for g in range(2):
                row = rows_of(place, y, g, place[2])
                keep[y, g, n] = grad[pl.ds(row, 32), :].astype(BF16)
                row = rows_of(place, y, g, 1 - place[2])
                send[y, g, n] = grad[pl.ds(row, 32), :].astype(BF16)


def core_sum_kernel(place, keep, got, out):
    out[...] = (keep[...].astype(F32) + got[...].astype(F32)).astype(BF16)


def group_sum_kernel(place, near, far, mine, send):
    total = far[0].astype(F32)
    for y in range(1, 4):
        total = total + far[y].astype(F32)
    mine[:3] = near[0].astype(F32)
    mine[3:] = total[0]
    send[:3] = near[1]
    send[3:] = total[1].astype(BF16)


def output_kernel(place, inputs, n0, n1, n2, n3, n4, w, st, low, out):
    total = dot_nt(st[:, :R], low[:, R:])
    for n, left in enumerate((inputs, n0, n1, n2, n3, n4)):
        total = total + dot_nn(left[...], w[n])
    out[...] = total.astype(BF16)


def grad_inputs_kernel(place, cot, w, z0, z1, z2, z3, z4, st, low, out):
    total = dot_nt(cot[...], w[0]) + dot_nt(st[:, R:], low[:, :R])
    for z in (z0, z1, z2, z3, z4):
        total = total + z[...].astype(F32)
    out[...] = total.astype(BF16)


def body(inputs, cotangent, butterfly, low_in, low_out):
    dp = lax.axis_index("dp")
    place = jnp.stack([dp // 4, (dp // 2) % 2, dp % 2, lax.axis_index("feat") % 4]).astype(jnp.int32)
    block = (256, BS)
    levels = LEVELS + 1

    shard = jnp.concatenate(
        [butterfly, jnp.concatenate([low_in, low_out.T], axis=1)[None]], axis=0
    )
    got = over_dp(shard, Z_HI)
    near = [over_feat(inputs, PARTNER[l]) for l in range(2)]
    (near_parts,) = call(
        near_grads_kernel, [((8, 2, 3, 32, BS), BF16)], place, inputs, *near, cotangent,
        scratch=[pltpu.VMEM((BS, BS), F32)], name="near_grads",
    )
    got = tie(got, near_parts)
    weights, low_pair = call(
        pair_kernel, [((2, levels, 32, BS), BF16), ((8, 2, 32, 2 * R), BF16)], place, shard, got,
        name="pair",
    )
    gathered = lax.all_gather(weights, "dp", axis_index_groups=YC_GROUPS)
    low_rows = exchange(low_pair, "dp", YC_GROUPS)
    z_inputs = tie(inputs, got)
    near += [over_feat(z_inputs, PARTNER[l]) for l in range(2, LEVELS)]
    low_rows = tie(low_rows, near[2])

    low, parts = call(
        project_kernel, [((BS, 2 * R), BF16), ((4, 64, 2 * R), BF16)],
        place, low_rows, inputs, cotangent,
        scratch=[pltpu.VMEM((256, 2 * R), F32)], name="project",
    )
    parts = tie(exchange(parts, "feat", X_GROUPS), near[3])
    (total,) = call(x_sum_kernel, [((64, 2 * R), BF16)], place, parts, name="x_sum")
    for level in (2, 3, 4):
        total = (total.astype(F32) + over_feat(total, PARTNER[level]).astype(F32)).astype(BF16)
    st = exchange(jnp.broadcast_to(total, (4, 64, 2 * R)), "feat", X_GROUPS)
    st = st.reshape(256, 2 * R)

    gathered = tie(gathered, total)
    near_parts = tie(near_parts, gathered)
    near_sum = lax.psum_scatter(near_parts, "dp", axis_index_groups=YC_GROUPS)
    *z, w = call(
        weights_kernel, [(block, BF16)] * LEVELS + [((levels, BS, BS), BF16)],
        place, gathered, cotangent, name="weights",
    )
    st = tie(st, w)
    z = [over_feat(z[l], PARTNER[l]) for l in reversed(range(LEVELS))][::-1]

    half = (4, 2, 4, 32, BS)
    keep, send = call(
        far_grads_kernel, [(half, BF16)] * 2, place, *near[2:], st, inputs, cotangent,
        scratch=[pltpu.VMEM((BS, BS), F32)], name="far_grads",
    )
    got = over_dp(send, CORE)
    (parts,) = call(core_sum_kernel, [(half, BF16)], place, keep, got, name="far_grads_core")
    w = tie(w, parts)
    (output,) = call(
        output_kernel, [(block, BF16)], place, inputs, *near, w, st, low, name="output"
    )
    parts = exchange(parts, "dp", Y_GROUPS)
    piece = (levels + 1, 32, BS)
    mine, send = call(
        group_sum_kernel, [(piece, F32), (piece, BF16)], place, near_sum, parts, name="grads_sum"
    )
    grads = (mine + over_dp(send, Z_HI).astype(F32)) * SCALE
    (grad_inputs,) = call(
        grad_inputs_kernel, [(block, BF16)], place, cotangent, w, *z, tie(st, send), low,
        name="grad_inputs",
    )
    return output, grad_inputs, grads[:levels], grads[levels, :, :R], grads[levels, :, R:].T


def solution(mesh):
    specs = (
        P("dp", "feat"),
        P("dp", "feat"),
        P(None, ("feat", "dp"), None),
        P(("feat", "dp"), None),
        P(None, ("feat", "dp")),
    )
    return jax.shard_map(body, mesh=mesh, in_specs=specs, out_specs=specs, check_vma=False)
```

```python
import functools

import jax
import jax.numpy as jnp
from jax import lax
from jax.experimental import pallas as pl
from jax.experimental.pallas import tpu as pltpu
from jax.sharding import PartitionSpec as P

BS = 512
LEVELS = 5
R = 256
SCALE = 1.0 / 64.0
F32 = jnp.float32
BF16 = jnp.bfloat16


def dp_pairs(step):
    pairs = []
    for i in range(16):
        y, h, c = step(i // 4, (i // 2) % 2, i % 2)
        pairs.append((i, (y * 2 + h) * 2 + c))
    return pairs


Z_HI = dp_pairs(lambda y, h, c: (y, 1 - h, c))
YC_GROUPS = [[(y * 2 + h) * 2 + c for y in range(4) for c in range(2)] for h in range(2)]
X_GROUPS = [[z * 4 + x for x in range(4)] for z in range(8)]
PARTNER = [[(i, i ^ (1 << level)) for i in range(32)] for level in range(LEVELS)]


def tie(value, *earlier):
    return lax.optimization_barrier((value, *earlier))[0]


def over_dp(value, pairs):
    return lax.ppermute(value, "dp", pairs)


def over_feat(value, pairs):
    return lax.ppermute(value, "feat", pairs)


def exchange(value, axis, groups):
    return lax.all_to_all(value, axis, 0, 0, tiled=True, axis_index_groups=groups)


def dot_nn(a, b):
    return lax.dot_general(a, b, (((1,), (0,)), ((), ())), preferred_element_type=F32)


def dot_nt(a, b):
    return lax.dot_general(a, b, (((1,), (1,)), ((), ())), preferred_element_type=F32)


def dot_tn(a, b):
    return lax.dot_general(a, b, (((0,), (0,)), ((), ())), preferred_element_type=F32)


def call(kernel, out, place, *args, scratch=(), name, limit=24):
    shapes = [jax.ShapeDtypeStruct(s, d) for s, d in out]
    return pl.pallas_call(
        kernel,
        out_shape=shapes,
        in_specs=[pl.BlockSpec(memory_space=pltpu.SMEM)]
        + [pl.BlockSpec(memory_space=pltpu.VMEM)] * len(args),
        out_specs=[pl.BlockSpec(memory_space=pltpu.VMEM)] * len(out),
        scratch_shapes=list(scratch),
        compiler_params=pltpu.CompilerParams(vmem_limit_bytes=limit << 20),
        name=name,
    )(place, *args)


def rows_of(place, y, g, c):
    h = lax.rem(place[1] + g, 2)
    return pl.multiple_of(((y * 2 + h) * 2 + c) * 32, 32)


def pair_kernel(place, mine, got, weights, low):
    weights[0] = mine[: LEVELS + 1]
    weights[1] = got[: LEVELS + 1]
    for k in range(8):
        low[k, 0] = mine[LEVELS + 1]
        low[k, 1] = got[LEVELS + 1]


def order_low(place, gathered, low):
    for k in range(8):
        for g in range(2):
            low[pl.ds(rows_of(place, k // 2, g, k % 2), 32), :] = gathered[k, g]


def project_kernel(place, gathered, inputs, cot, out, low, part):
    order_low(place, gathered, low)
    part[:, :R] = dot_nn(inputs[...], low[:, :R])
    part[:, R:] = dot_nn(cot[...], low[:, R:])
    for x in range(4):
        out[x] = part[x * 64 : (x + 1) * 64, :].astype(BF16)


def weights_kernel(place, gathered, cot, z4, z3, z2, z1, z0, w):
    for k in range(8):
        for g in range(2):
            w[:, pl.ds(rows_of(place, k // 2, g, k % 2), 32), :] = gathered[k, g]
    for level, z in enumerate((z0, z1, z2, z3, z4)):
        z[...] = dot_nt(cot[...], w[level + 1]).astype(BF16)


def x_sum_kernel(place, parts, out):
    total = parts[0].astype(F32)
    for x in range(1, 4):
        total = total + parts[x].astype(F32)
    out[...] = total.astype(BF16)


def near_grads_kernel(place, inputs, n0, n1, n2, cot, out, grad):
    for n, left in enumerate((inputs, n0, n1, n2)):
        grad[...] = dot_tn(left[...], cot[...])
        for k in range(8):
            for g in range(2):
                row = rows_of(place, k // 2, g, k % 2)
                out[k, g, n] = grad[pl.ds(row, 32), :].astype(BF16)


def far_grads_kernel(place, n3, n4, st, inputs, cot, out, grad):
    for n, left in enumerate((n3, n4, None)):
        if left is None:
            grad[:, :R] = dot_tn(inputs[...], st[:, R:])
            grad[:, R:] = dot_tn(cot[...], st[:, :R])
        else:
            grad[...] = dot_tn(left[...], cot[...])
        for k in range(8):
            for g in range(2):
                row = rows_of(place, k // 2, g, k % 2)
                out[k, g, n] = grad[pl.ds(row, 32), :].astype(BF16)


def group_sum_kernel(place, near, far, mine, send):
    total = far[0].astype(F32)
    for k in range(1, 8):
        total = total + far[k].astype(F32)
    mine[:4] = near[0].astype(F32)
    mine[4:] = total[0]
    send[:4] = near[1]
    send[4:] = total[1].astype(BF16)


def output_kernel(place, inputs, n0, n1, n2, n3, n4, w, st, gathered, out, low):
    order_low(place, gathered, low)
    total = dot_nt(st[:, :R], low[:, R:])
    for n, left in enumerate((inputs, n0, n1, n2, n3, n4)):
        total = total + dot_nn(left[...], w[n])
    out[...] = total.astype(BF16)


def grad_inputs_kernel(place, cot, w, z4, z3, z2, z1, z0, st, gathered, out, low):
    order_low(place, gathered, low)
    total = dot_nt(cot[...], w[0]) + dot_nt(st[:, R:], low[:, :R])
    for z in (z4, z3, z2, z1, z0):
        total = total + z[...].astype(F32)
    out[...] = total.astype(BF16)


def body(inputs, cotangent, butterfly, low_in, low_out):
    dp = lax.axis_index("dp")
    place = jnp.stack([dp // 4, (dp // 2) % 2, dp % 2, lax.axis_index("feat") % 4]).astype(jnp.int32)
    block = (256, BS)
    levels = LEVELS + 1

    shard = jnp.concatenate(
        [butterfly, jnp.concatenate([low_in, low_out.T], axis=1)[None]], axis=0
    )
    got = over_dp(shard, Z_HI)
    near = [over_feat(inputs, PARTNER[l]) for l in range(3)]
    (near_parts,) = call(
        near_grads_kernel, [((8, 2, 4, 32, BS), BF16)], place, inputs, *near, cotangent,
        scratch=[pltpu.VMEM((BS, BS), F32)], name="near_grads",
    )
    got = tie(got, near_parts)
    weights, low_pair = call(
        pair_kernel, [((2, levels, 32, BS), BF16), ((8, 2, 32, 2 * R), BF16)], place, shard, got,
        name="pair",
    )
    gathered = lax.all_gather(weights, "dp", axis_index_groups=YC_GROUPS)
    low_rows = exchange(low_pair, "dp", YC_GROUPS)
    z_inputs = tie(inputs, got)
    near += [over_feat(z_inputs, PARTNER[l]) for l in range(3, LEVELS)]
    (parts,) = call(
        project_kernel, [((4, 64, 2 * R), BF16)], place, low_rows, inputs, cotangent,
        scratch=[pltpu.VMEM((BS, 2 * R), BF16), pltpu.VMEM((256, 2 * R), F32)], name="project",
    )
    parts = tie(exchange(parts, "feat", X_GROUPS), near[4])
    (total,) = call(x_sum_kernel, [((64, 2 * R), BF16)], place, parts, name="x_sum")
    near_parts = tie(near_parts, total)
    for level in (2, 3, 4):
        total = (total.astype(F32) + over_feat(total, PARTNER[level]).astype(F32)).astype(BF16)
    near_sum = lax.psum_scatter(near_parts, "dp", axis_index_groups=YC_GROUPS)

    st = exchange(jnp.broadcast_to(total, (4, 64, 2 * R)), "feat", X_GROUPS)
    st = st.reshape(256, 2 * R)

    gathered = tie(gathered, total)
    *z, w = call(
        weights_kernel, [(block, BF16)] * LEVELS + [((levels, BS, BS), BF16)],
        place, gathered, cotangent, name="weights", limit=60,
    )
    z = z[::-1]
    z = [over_feat(z[l], PARTNER[l]) for l in reversed(range(LEVELS))][::-1]
    st = tie(st, w)

    (parts,) = call(
        far_grads_kernel, [((8, 2, 3, 32, BS), BF16)], place, *near[3:], st, inputs, cotangent,
        scratch=[pltpu.VMEM((BS, BS), F32)], name="far_grads",
    )
    w = tie(w, parts)
    (output,) = call(
        output_kernel, [(block, BF16)], place, inputs, *near, w, st, low_rows,
        scratch=[pltpu.VMEM((BS, 2 * R), BF16)], name="output",
    )
    parts = exchange(parts, "dp", YC_GROUPS)
    piece = (levels + 1, 32, BS)
    mine, send = call(
        group_sum_kernel, [(piece, F32), (piece, BF16)], place, near_sum, parts, name="grads_sum"
    )
    grads = (mine + over_dp(send, Z_HI).astype(F32)) * SCALE
    (grad_inputs,) = call(
        grad_inputs_kernel, [(block, BF16)], place, cotangent, w, *z[::-1], tie(st, send), low_rows,
        scratch=[pltpu.VMEM((BS, 2 * R), BF16)], name="grad_inputs",
    )
    return output, grad_inputs, grads[:levels], grads[levels, :, :R], grads[levels, :, R:].T


def solution(mesh):
    specs = (
        P("dp", "feat"),
        P("dp", "feat"),
        P(None, ("feat", "dp"), None),
        P(("feat", "dp"), None),
        P(None, ("feat", "dp")),
    )
    return jax.shard_map(body, mesh=mesh, in_specs=specs, out_specs=specs, check_vma=False)
```

```python
import functools

import jax
import jax.numpy as jnp
from jax import lax
from jax.experimental import pallas as pl
from jax.experimental.pallas import tpu as pltpu
from jax.sharding import PartitionSpec as P

BS = 512
LEVELS = 5
R = 256
SCALE = 1.0 / 64.0
F32 = jnp.float32
BF16 = jnp.bfloat16


def dp_pairs(step):
    pairs = []
    for i in range(16):
        y, h, c = step(i // 4, (i // 2) % 2, i % 2)
        pairs.append((i, (y * 2 + h) * 2 + c))
    return pairs


Z_HI = dp_pairs(lambda y, h, c: (y, 1 - h, c))
YC_GROUPS = [[(y * 2 + h) * 2 + c for y in range(4) for c in range(2)] for h in range(2)]
X_GROUPS = [[z * 4 + x for x in range(4)] for z in range(8)]
Z_GROUPS = [[(z + i) * 4 + x for i in range(4)] for z in (0, 4) for x in range(4)]
PARTNER = [[(i, i ^ (1 << level)) for i in range(32)] for level in range(LEVELS)]


def tie(value, *earlier):
    return lax.optimization_barrier((value, *earlier))[0]


def over_dp(value, pairs):
    return lax.ppermute(value, "dp", pairs)


def over_feat(value, pairs):
    return lax.ppermute(value, "feat", pairs)


def exchange(value, axis, groups):
    return lax.all_to_all(value, axis, 0, 0, tiled=True, axis_index_groups=groups)


def dot_nn(a, b):
    return lax.dot_general(a, b, (((1,), (0,)), ((), ())), preferred_element_type=F32)


def dot_nt(a, b):
    return lax.dot_general(a, b, (((1,), (1,)), ((), ())), preferred_element_type=F32)


def dot_tn(a, b):
    return lax.dot_general(a, b, (((0,), (0,)), ((), ())), preferred_element_type=F32)


def call(kernel, out, place, *args, scratch=(), name, limit=24):
    shapes = [jax.ShapeDtypeStruct(s, d) for s, d in out]
    return pl.pallas_call(
        kernel,
        out_shape=shapes,
        in_specs=[pl.BlockSpec(memory_space=pltpu.SMEM)]
        + [pl.BlockSpec(memory_space=pltpu.VMEM)] * len(args),
        out_specs=[pl.BlockSpec(memory_space=pltpu.VMEM)] * len(out),
        scratch_shapes=list(scratch),
        compiler_params=pltpu.CompilerParams(vmem_limit_bytes=limit << 20),
        name=name,
    )(place, *args)


def rows_of(place, y, g, c):
    h = lax.rem(place[1] + g, 2)
    return pl.multiple_of(((y * 2 + h) * 2 + c) * 32, 32)


def pair_kernel(place, mine, got, weights, low):
    weights[0] = mine[: LEVELS + 1]
    weights[1] = got[: LEVELS + 1]
    for k in range(8):
        low[k, 0] = mine[LEVELS + 1]
        low[k, 1] = got[LEVELS + 1]


def order_low(place, gathered, low):
    for k in range(8):
        for g in range(2):
            low[pl.ds(rows_of(place, k // 2, g, k % 2), 32), :] = gathered[k, g]


def project_kernel(place, gathered, inputs, cot, out, low, part):
    order_low(place, gathered, low)
    part[:, :R] = dot_nn(inputs[...], low[:, :R])
    part[:, R:] = dot_nn(cot[...], low[:, R:])
    for x in range(4):
        out[x] = part[x * 64 : (x + 1) * 64, :].astype(BF16)


def far_weights_kernel(place, gathered, cot, z4, z3, z2, w):
    for k in range(8):
        for g in range(2):
            rows = pl.ds(rows_of(place, k // 2, g, k % 2), 32)
            w[:, rows, :] = gathered[k, g, 3:]
    for level, z in enumerate((z2, z3, z4)):
        z[...] = dot_nt(cot[...], w[level]).astype(BF16)


def near_weights_kernel(place, gathered, cot, z1, z0, w):
    for k in range(8):
        for g in range(2):
            rows = pl.ds(rows_of(place, k // 2, g, k % 2), 32)
            w[:, rows, :] = gathered[k, g, :3]
    for level, z in enumerate((z0, z1)):
        z[...] = dot_nt(cot[...], w[level + 1]).astype(BF16)


def sum_kernel(place, parts, out):
    total = parts[0].astype(F32)
    for k in range(1, parts.shape[0]):
        total = total + parts[k].astype(F32)
    for k in range(out.shape[0]):
        out[k] = total.astype(BF16)


def pair_sum_kernel(place, mine, got, out):
    total = mine[0].astype(F32) + got[0].astype(F32)
    for k in range(out.shape[0]):
        out[k] = total.astype(BF16)


def near_grads_kernel(place, inputs, n0, n1, n2, cot, out, grad):
    for n, left in enumerate((inputs, n0, n1, n2)):
        grad[...] = dot_tn(left[...], cot[...])
        for k in range(8):
            for g in range(2):
                row = rows_of(place, k // 2, g, k % 2)
                out[k, g, n] = grad[pl.ds(row, 32), :].astype(BF16)


def far_grads_kernel(place, n3, n4, st, inputs, cot, out, grad):
    for n, left in enumerate((n3, n4, None)):
        if left is None:
            grad[:, :R] = dot_tn(inputs[...], st[:, R:])
            grad[:, R:] = dot_tn(cot[...], st[:, :R])
        else:
            grad[...] = dot_tn(left[...], cot[...])
        for k in range(8):
            for g in range(2):
                row = rows_of(place, k // 2, g, k % 2)
                out[k, g, n] = grad[pl.ds(row, 32), :].astype(BF16)


def group_sum_kernel(place, near, far, mine, send):
    total = far[0].astype(F32)
    for k in range(1, 8):
        total = total + far[k].astype(F32)
    mine[:4] = near[0].astype(F32)
    mine[4:] = total[0]
    send[:4] = near[1]
    send[4:] = total[1].astype(BF16)


def output_kernel(
    place, inputs, n0, n1, n2, n3, n4, near_w, far_w, st, gathered, out, low
):
    order_low(place, gathered, low)
    total = dot_nt(st[:, :R], low[:, R:])
    for n, left in enumerate((inputs, n0, n1, n2, n3, n4)):
        total = total + dot_nn(left[...], near_w[n] if n < 3 else far_w[n - 3])
    out[...] = total.astype(BF16)


def grad_inputs_kernel(place, cot, w, z4, z3, z2, z1, z0, st, gathered, out, low):
    order_low(place, gathered, low)
    total = dot_nt(cot[...], w[0]) + dot_nt(st[:, R:], low[:, :R])
    for z in (z4, z3, z2, z1, z0):
        total = total + z[...].astype(F32)
    out[...] = total.astype(BF16)


def body(inputs, cotangent, butterfly, low_in, low_out):
    dp = lax.axis_index("dp")
    place = jnp.stack([dp // 4, (dp // 2) % 2, dp % 2, lax.axis_index("feat") % 4]).astype(jnp.int32)
    block = (256, BS)
    levels = LEVELS + 1

    shard = jnp.concatenate(
        [butterfly, jnp.concatenate([low_in, low_out.T], axis=1)[None]], axis=0
    )
    got = over_dp(shard, Z_HI)
    near = [over_feat(inputs, PARTNER[l]) for l in range(3)]
    (near_parts,) = call(
        near_grads_kernel, [((8, 2, 4, 32, BS), BF16)], place, inputs, *near, cotangent,
        scratch=[pltpu.VMEM((BS, BS), F32)], name="near_grads",
    )
    got = tie(got, near_parts)
    weights, low_pair = call(
        pair_kernel, [((2, levels, 32, BS), BF16), ((8, 2, 32, 2 * R), BF16)], place, shard, got,
        name="pair",
    )
    gathered = lax.all_gather(weights, "dp", axis_index_groups=YC_GROUPS)
    low_rows = exchange(low_pair, "dp", YC_GROUPS)
    z_inputs = tie(inputs, got)
    near += [over_feat(z_inputs, PARTNER[l]) for l in range(3, LEVELS)]
    (parts,) = call(
        project_kernel, [((4, 64, 2 * R), BF16)], place, low_rows, inputs, cotangent,
        scratch=[pltpu.VMEM((BS, 2 * R), BF16), pltpu.VMEM((256, 2 * R), F32)], name="project",
    )
    parts = tie(exchange(parts, "feat", X_GROUPS), near[4])
    (parts,) = call(sum_kernel, [((4, 64, 2 * R), BF16)], place, parts, name="x_sum")
    near_parts = tie(near_parts, parts)
    parts = exchange(parts, "feat", Z_GROUPS)
    (total,) = call(sum_kernel, [((1, 64, 2 * R), BF16)], place, parts, name="z_sum")
    (parts,) = call(
        pair_sum_kernel, [((4, 64, 2 * R), BF16)], place, total, over_feat(total, PARTNER[4]),
        name="last_sum",
    )
    near_sum = lax.psum_scatter(near_parts, "dp", axis_index_groups=YC_GROUPS)

    st = exchange(parts, "feat", X_GROUPS)
    st = st.reshape(256, 2 * R)

    gathered = tie(gathered, parts)
    *far_z, far_w = call(
        far_weights_kernel, [(block, BF16)] * 3 + [((3, BS, BS), BF16)],
        place, gathered, cotangent, name="far_weights", limit=60,
    )
    far_z = [over_feat(far_z[4 - l], PARTNER[l]) for l in (4, 3, 2)][::-1]
    st = tie(st, far_w)

    (parts,) = call(
        far_grads_kernel, [((8, 2, 3, 32, BS), BF16)], place, *near[3:], st, inputs, cotangent,
        scratch=[pltpu.VMEM((BS, BS), F32)], name="far_grads",
    )
    *near_z, near_w = call(
        near_weights_kernel, [(block, BF16)] * 2 + [((3, BS, BS), BF16)],
        place, tie(gathered, parts), cotangent, name="near_weights", limit=60,
    )
    z = [over_feat(near_z[1 - l], PARTNER[l]) for l in (1, 0)][::-1] + far_z
    (output,) = call(
        output_kernel, [(block, BF16)], place, inputs, *near, near_w, far_w, st, low_rows,
        scratch=[pltpu.VMEM((BS, 2 * R), BF16)], name="output",
    )
    parts = exchange(parts, "dp", YC_GROUPS)
    piece = (levels + 1, 32, BS)
    mine, send = call(
        group_sum_kernel, [(piece, F32), (piece, BF16)], place, near_sum, parts, name="grads_sum"
    )
    grads = (mine + over_dp(send, Z_HI).astype(F32)) * SCALE
    (grad_inputs,) = call(
        grad_inputs_kernel, [(block, BF16)], place, cotangent, near_w, *z[::-1], tie(st, send), low_rows,
        scratch=[pltpu.VMEM((BS, 2 * R), BF16)], name="grad_inputs",
    )
    return output, grad_inputs, grads[:levels], grads[levels, :, :R], grads[levels, :, R:].T


def solution(mesh):
    specs = (
        P("dp", "feat"),
        P("dp", "feat"),
        P(None, ("feat", "dp"), None),
        P(("feat", "dp"), None),
        P(None, ("feat", "dp")),
    )
    return jax.shard_map(body, mesh=mesh, in_specs=specs, out_specs=specs, check_vma=False)
```

```python
import functools

import jax
import jax.numpy as jnp
from jax import lax
from jax.experimental import pallas as pl
from jax.experimental.pallas import tpu as pltpu
from jax.sharding import PartitionSpec as P

BS = 512
LEVELS = 5
R = 256
SCALE = 1.0 / 64.0
F32 = jnp.float32
BF16 = jnp.bfloat16


def dp_pairs(step):
    pairs = []
    for i in range(16):
        y, h, c = step(i // 4, (i // 2) % 2, i % 2)
        pairs.append((i, (y * 2 + h) * 2 + c))
    return pairs


Z_HI = dp_pairs(lambda y, h, c: (y, 1 - h, c))
YC_GROUPS = [[(y * 2 + h) * 2 + c for y in range(4) for c in range(2)] for h in range(2)]
X_GROUPS = [[z * 4 + x for x in range(4)] for z in range(8)]
Z_GROUPS = [[(z + i) * 4 + x for i in range(4)] for z in (0, 4) for x in range(4)]
PARTNER = [[(i, i ^ (1 << level)) for i in range(32)] for level in range(LEVELS)]


def tie(value, *earlier):
    return lax.optimization_barrier((value, *earlier))[0]


def over_dp(value, pairs):
    return lax.ppermute(value, "dp", pairs)


def over_feat(value, pairs):
    return lax.ppermute(value, "feat", pairs)


def exchange(value, axis, groups):
    return lax.all_to_all(value, axis, 0, 0, tiled=True, axis_index_groups=groups)


def dot_nn(a, b):
    return lax.dot_general(a, b, (((1,), (0,)), ((), ())), preferred_element_type=F32)


def dot_nt(a, b):
    return lax.dot_general(a, b, (((1,), (1,)), ((), ())), preferred_element_type=F32)


def dot_tn(a, b):
    return lax.dot_general(a, b, (((0,), (0,)), ((), ())), preferred_element_type=F32)


def call(kernel, out, place, *args, scratch=(), name, limit=24, part=None):
    shapes = [jax.ShapeDtypeStruct(s, d) for s, d in out]
    specs = [pl.BlockSpec(memory_space=pltpu.VMEM)] * len(args)
    if part is not None:
        specs[0] = pl.BlockSpec((8, 2, 3, 32, BS), lambda _: (0, 0, part, 0, 0))
    return pl.pallas_call(
        kernel,
        out_shape=shapes,
        in_specs=[pl.BlockSpec(memory_space=pltpu.SMEM)]
        + specs,
        grid=() if part is None else (1,),
        out_specs=[pl.BlockSpec(memory_space=pltpu.VMEM)] * len(out),
        scratch_shapes=list(scratch),
        compiler_params=pltpu.CompilerParams(vmem_limit_bytes=limit << 20),
        name=name,
    )(place, *args)


def rows_of(place, y, g, c):
    h = lax.rem(place[1] + g, 2)
    return pl.multiple_of(((y * 2 + h) * 2 + c) * 32, 32)


def pair_kernel(place, mine, got, weights, low):
    weights[0] = mine[: LEVELS + 1]
    weights[1] = got[: LEVELS + 1]
    for k in range(8):
        low[k, 0] = mine[LEVELS + 1]
        low[k, 1] = got[LEVELS + 1]


def order_low(place, gathered, low):
    for k in range(8):
        for g in range(2):
            low[pl.ds(rows_of(place, k // 2, g, k % 2), 32), :] = gathered[k, g]


def project_kernel(place, gathered, inputs, cot, out, low, part):
    order_low(place, gathered, low)
    part[:, :R] = dot_nn(inputs[...], low[:, :R])
    part[:, R:] = dot_nn(cot[...], low[:, R:])
    for x in range(4):
        out[x] = part[x * 64 : (x + 1) * 64, :].astype(BF16)


def far_weights_kernel(place, gathered, cot, z4, z3, z2, w):
    for k in range(8):
        for g in range(2):
            rows = pl.ds(rows_of(place, k // 2, g, k % 2), 32)
            w[:, rows, :] = gathered[k, g]
    for level, z in enumerate((z2, z3, z4)):
        z[...] = dot_nt(cot[...], w[level]).astype(BF16)


def near_weights_kernel(place, gathered, cot, z1, z0, w):
    for k in range(8):
        for g in range(2):
            rows = pl.ds(rows_of(place, k // 2, g, k % 2), 32)
            w[:, rows, :] = gathered[k, g]
    for level, z in enumerate((z0, z1)):
        z[...] = dot_nt(cot[...], w[level + 1]).astype(BF16)


def sum_kernel(place, parts, out):
    total = parts[0].astype(F32)
    for k in range(1, parts.shape[0]):
        total = total + parts[k].astype(F32)
    for k in range(out.shape[0]):
        out[k] = total.astype(BF16)


def pair_sum_kernel(place, mine, got, out):
    total = mine[0].astype(F32) + got[0].astype(F32)
    for k in range(out.shape[0]):
        out[k] = total.astype(BF16)


def near_grads_kernel(place, inputs, n0, n1, n2, cot, out, grad):
    for n, left in enumerate((inputs, n0, n1, n2)):
        grad[...] = dot_tn(left[...], cot[...])
        for k in range(8):
            for g in range(2):
                row = rows_of(place, k // 2, g, k % 2)
                out[k, g, n] = grad[pl.ds(row, 32), :].astype(BF16)


def far_grads_kernel(place, n3, n4, st, inputs, cot, out, grad):
    for n, left in enumerate((n3, n4, None)):
        if left is None:
            grad[:, :R] = dot_tn(inputs[...], st[:, R:])
            grad[:, R:] = dot_tn(cot[...], st[:, :R])
        else:
            grad[...] = dot_tn(left[...], cot[...])
        for k in range(8):
            for g in range(2):
                row = rows_of(place, k // 2, g, k % 2)
                out[k, g, n] = grad[pl.ds(row, 32), :].astype(BF16)


def group_sum_kernel(place, near, far, mine, send):
    total = far[0].astype(F32)
    for k in range(1, 8):
        total = total + far[k].astype(F32)
    mine[:4] = near[0].astype(F32)
    mine[4:] = total[0]
    send[:4] = near[1]
    send[4:] = total[1].astype(BF16)


def output_kernel(
    place, inputs, n0, n1, n2, n3, n4, near_w, far_w, st, gathered, out, low
):
    order_low(place, gathered, low)
    total = dot_nt(st[:, :R], low[:, R:])
    for n, left in enumerate((inputs, n0, n1, n2, n3, n4)):
        total = total + dot_nn(left[...], near_w[n] if n < 3 else far_w[n - 3])
    out[...] = total.astype(BF16)


def grad_inputs_kernel(place, cot, w, z4, z3, z2, z1, z0, st, gathered, out, low):
    order_low(place, gathered, low)
    total = dot_nt(cot[...], w[0]) + dot_nt(st[:, R:], low[:, :R])
    for z in (z4, z3, z2, z1, z0):
        total = total + z[...].astype(F32)
    out[...] = total.astype(BF16)


def body(inputs, cotangent, butterfly, low_in, low_out):
    dp = lax.axis_index("dp")
    place = jnp.stack([dp // 4, (dp // 2) % 2, dp % 2, lax.axis_index("feat") % 4]).astype(jnp.int32)
    block = (256, BS)
    levels = LEVELS + 1

    shard = jnp.concatenate(
        [butterfly, jnp.concatenate([low_in, low_out.T], axis=1)[None]], axis=0
    )
    got = over_dp(shard, Z_HI)
    near = [over_feat(inputs, PARTNER[l]) for l in range(3)]
    (near_parts,) = call(
        near_grads_kernel, [((8, 2, 4, 32, BS), BF16)], place, inputs, *near, cotangent,
        scratch=[pltpu.VMEM((BS, BS), F32)], name="near_grads",
    )
    got = tie(got, near_parts)
    weights, low_pair = call(
        pair_kernel, [((2, levels, 32, BS), BF16), ((8, 2, 32, 2 * R), BF16)], place, shard, got,
        name="pair",
    )
    gathered = lax.all_gather(weights, "dp", axis_index_groups=YC_GROUPS)
    low_rows = exchange(low_pair, "dp", YC_GROUPS)
    z_inputs = tie(inputs, got)
    near += [over_feat(z_inputs, PARTNER[l]) for l in range(3, LEVELS)]
    (parts,) = call(
        project_kernel, [((4, 64, 2 * R), BF16)], place, low_rows, inputs, cotangent,
        scratch=[pltpu.VMEM((BS, 2 * R), BF16), pltpu.VMEM((256, 2 * R), F32)], name="project",
    )
    parts = tie(exchange(parts, "feat", X_GROUPS), near[4])
    (parts,) = call(sum_kernel, [((4, 64, 2 * R), BF16)], place, parts, name="x_sum")
    near_parts = tie(near_parts, parts)
    parts = exchange(parts, "feat", Z_GROUPS)
    (total,) = call(sum_kernel, [((1, 64, 2 * R), BF16)], place, parts, name="z_sum")
    (parts,) = call(
        pair_sum_kernel, [((4, 64, 2 * R), BF16)], place, total, over_feat(total, PARTNER[4]),
        name="last_sum",
    )
    near_sum = lax.psum_scatter(near_parts, "dp", axis_index_groups=YC_GROUPS)

    st = exchange(parts, "feat", X_GROUPS)
    st = st.reshape(256, 2 * R)

    gathered = tie(gathered, parts)
    *far_z, far_w = call(
        far_weights_kernel, [(block, BF16)] * 3 + [((3, BS, BS), BF16)],
        place, gathered, cotangent, name="far_weights", limit=60, part=1,
    )
    far_z = [over_feat(far_z[4 - l], PARTNER[l]) for l in (4, 3, 2)][::-1]
    st = tie(st, far_w)

    (parts,) = call(
        far_grads_kernel, [((8, 2, 3, 32, BS), BF16)], place, *near[3:], st, inputs, cotangent,
        scratch=[pltpu.VMEM((BS, BS), F32)], name="far_grads",
    )
    *near_z, near_w = call(
        near_weights_kernel, [(block, BF16)] * 2 + [((3, BS, BS), BF16)],
        place, tie(gathered, parts), cotangent, name="near_weights", limit=60, part=0,
    )
    z = [over_feat(near_z[1 - l], PARTNER[l]) for l in (1, 0)][::-1] + far_z
    (output,) = call(
        output_kernel, [(block, BF16)], place, inputs, *near, near_w, far_w, st, low_rows,
        scratch=[pltpu.VMEM((BS, 2 * R), BF16)], name="output",
    )
    parts = exchange(parts, "dp", YC_GROUPS)
    piece = (levels + 1, 32, BS)
    mine, send = call(
        group_sum_kernel, [(piece, F32), (piece, BF16)], place, near_sum, parts, name="grads_sum"
    )
    grads = (mine + over_dp(send, Z_HI).astype(F32)) * SCALE
    (grad_inputs,) = call(
        grad_inputs_kernel, [(block, BF16)], place, cotangent, near_w, *z[::-1], tie(st, send), low_rows,
        scratch=[pltpu.VMEM((BS, 2 * R), BF16)], name="grad_inputs",
    )
    return output, grad_inputs, grads[:levels], grads[levels, :, :R], grads[levels, :, R:].T


def solution(mesh):
    specs = (
        P("dp", "feat"),
        P("dp", "feat"),
        P(None, ("feat", "dp"), None),
        P(("feat", "dp"), None),
        P(None, ("feat", "dp")),
    )
    return jax.shard_map(body, mesh=mesh, in_specs=specs, out_specs=specs, check_vma=False)
```
